512 devices in a mesh: replica: 32 (over x, z_lo, core), tensor: 16 (over z_hi, y).
Axes of the slice: x: 4, y: 4, z: 16 (z_hi: 4, z_lo: 4; z = z_hi * 4 + z_lo), core: 2. Of those that a mesh axis runs over, the one named last changes fastest.
Arguments:
- hidden_in: bfloat16 [4, 256, 2560], P(None, 'replica', 'tensor'), may hold values from -1500 to 1500
- norm_gain: float32 [2560], replicated, may hold values from 0.1 to 1.9
- w_query: bfloat16 [2560, 4096], P(None, 'tensor'), may hold values from -0.125 to 0.125
- w_keyval: bfloat16 [1024, 2560], P('tensor'), may hold values from -0.5 to 0.5
- w_out: bfloat16 [4096, 2560], P('tensor'), may hold values from -0.1875 to 0.1875
- query_input_factor: bfloat16 [64, 2560], P('replica'), may hold values from -0.125 to 0.125
- b_query: bfloat16 [64, 4096], P('replica', 'tensor'), may hold values from -0.25976562 to 0.25976562
- a_out: bfloat16 [64, 4096], P('replica', 'tensor'), may hold values from -0.1875 to 0.1875
- b_out: bfloat16 [64, 2560], P('replica'), may hold values from -0.25976562 to 0.25976562
- component_owner_rows: int32 [2, 64], replicated, may hold values from 0 to 63, each once within a row
- lengths: int32 [256], P('replica'), may hold values from 256 to 2048, as said below
- kv_cache: bfloat16 [256, 2048, 1024], P('replica', 'tensor'), may hold values from -1700 to 1700
Outputs:
- attention_out: bfloat16 [4, 256, 2560], P(None, 'replica', 'tensor')
The draws below stay inside these ranges and needn't reach their ends.
Inputs may be any that keep to these rules, and one draw needn't show every extreme that they name: Positions lengths[b] and beyond of sequence b are unused; some sequence fills all 2048 positions.
All inputs are finite; a program needn't handle non-finite values.
Results may differ from the reference program's by a relative error of at most 0.02.
The reference program's roundings to bfloat16 on the way count: a program that leaves them out, or rounds other values in their place, can miss the bound.
Values may be sent and summed in bfloat16 or wider, within the bound.
A program may use at most 64 MiB of HBM per device.

```python
import math
import jax
import jax.numpy as jnp
from jax import lax

D = 2560
HQ = 32
KVH = 4
HD = 128
ADAPTER_RANK = 64
STEPS = 4
SEQ_DEV = 8
CACHE = 2048
SEQS = 256
N_TENSOR = 16


def draw_hidden_in(key, part):
    key = jax.random.fold_in(key, 11)
    noise_key, row_key, column_key = jax.random.split(key, 3)
    array_shape = (STEPS, SEQS, D)
    values = jnp.clip(jax.random.normal(noise_key, array_shape, jnp.float32), -6.0, 6.0)
    row_scale = jnp.exp(jax.random.uniform(row_key, (STEPS, SEQS, 1), jnp.float32, 0.0, math.log(10.0)))
    column_scale = jnp.exp(jax.random.uniform(column_key, (D,), jnp.float32, 0.0, math.log(10.0)))
    return (values * row_scale * column_scale).astype(jnp.bfloat16)


def draw_lengths(key, part):
    key = jax.random.fold_in(key, 23)
    length_key, chosen_key = jax.random.split(key, 2)
    drawn = jax.random.randint(length_key, (SEQS,), CACHE // 8, CACHE + 1)
    chosen = jax.random.randint(chosen_key, (), 0, SEQS)
    label_names = jnp.arange(SEQS, dtype=jnp.int32)
    return jnp.where(label_names == chosen, CACHE, drawn).astype(jnp.int32)


def draw_kv_cache(key, part):
    key = jax.random.fold_in(key, 37)
    key_noise, value_noise = jax.random.split(key, 2)
    array_shape = (SEQS, CACHE, KVH * HD)
    keys = jnp.clip(jax.random.normal(key_noise, array_shape, jnp.float32), -6.0, 6.0) * 2.0
    values = jnp.clip(jax.random.normal(value_noise, array_shape, jnp.float32), -6.0, 6.0)
    return jnp.concatenate([keys, values], axis=2).astype(jnp.bfloat16)


def shard_levels(rng, shape, shards, smallest, largest):
    def one(dim, blocks):
        heights = jax.random.uniform(jax.random.fold_in(jax.random.fold_in(rng, 6), dim), (blocks,), jnp.float32, smallest / len(shards), largest / len(shards))
        return jnp.repeat(jnp.exp(heights), shape[dim] // blocks).reshape((-1,) + (1,) * (len(shape) - dim - 1))

    factor_of = one(*shards[0])
    for cut in shards[1:]:
        factor_of = factor_of * one(*cut)
    return factor_of


def normal_values(rng, dims, scale, reach, pieces=(), kind=jnp.bfloat16):
    values = jax.random.normal(rng, dims, jnp.float32) * scale
    if len(pieces) > 0:
        values = shard_levels(rng, dims, pieces, -0.22, 0.18) * values
    return jnp.clip(values, min=-reach, max=reach).astype(kind)


def setup_inputs(seed: int = 0) -> dict:
    seeds = jax.random.split(jax.random.key(seed), 13)
    hidden_in = draw_hidden_in(jax.random.fold_in(seeds[12], 71), 0)
    norm_gain = jnp.clip(1.0 + 0.18 * jax.random.normal(seeds[1], (D,), jnp.float32), 0.1, 1.9)
    w_query = normal_values(seeds[2], (D, HQ * HD), D ** -0.5, 0.125, ((1, 16),))
    w_keyval = normal_values(seeds[3], (2 * KVH * HD, D), (D // 16) ** -0.5, 0.5, ((0, 16),))
    w_out = normal_values(seeds[4], (HQ * HD, D), (HQ * HD // 4) ** -0.5, 0.1875, ((0, 16),))
    query_input_factor = normal_values(seeds[5], (ADAPTER_RANK, D), D ** -0.5, 0.125, ((0, 32),))
    b_query = normal_values(seeds[6], (ADAPTER_RANK, HQ * HD), 0.044, 0.25976562, ((0, 32), (1, 16)))
    a_out = normal_values(seeds[7], (ADAPTER_RANK, HQ * HD), (HQ * HD // 4) ** -0.5, 0.1875, ((0, 32), (1, 16)))
    b_out = normal_values(seeds[8], (ADAPTER_RANK, D), 0.044, 0.25976562, ((0, 32),))
    component_owner_rows = jax.vmap(lambda own: jax.random.permutation(own, ADAPTER_RANK))(jax.random.split(seeds[9], 2)).reshape((2, ADAPTER_RANK)).astype(jnp.int32)
    lengths = draw_lengths(jax.random.fold_in(seeds[12], 71), 0)
    kv_cache = draw_kv_cache(jax.random.fold_in(seeds[12], 71), 0)
    return {"hidden_in": hidden_in, "norm_gain": norm_gain, "w_query": w_query, "w_keyval": w_keyval, "w_out": w_out, "query_input_factor": query_input_factor, "b_query": b_query, "a_out": a_out, "b_out": b_out, "component_owner_rows": component_owner_rows, "lengths": lengths, "kv_cache": kv_cache}


adapter_scale = 2.0
norm_eps = 1e-06
masked_score = -1e+30
highest = lax.Precision.HIGHEST

def pairing_order(component_owner_rows, adapter_rank_size):
    label_names = lax.broadcasted_iota(jnp.int32, (adapter_rank_size, adapter_rank_size), 1)
    first_rows = (component_owner_rows[0][:, None] == label_names).astype(jnp.float32)
    second_rows = (component_owner_rows[1][:, None] == label_names).astype(jnp.float32)
    return jnp.dot(first_rows.T, second_rows, precision=highest)

def attend(operands):
    head_rows, appended, cached, limits = operands
    score_scale = HD ** (-0.5)
    blocks = N_TENSOR
    width = CACHE // N_TENSOR
    queries = head_rows.astype(jnp.float32)
    cache_keys = cached[:, :, 0].astype(jnp.float32)
    cache_values = cached[:, :, 1].astype(jnp.float32).reshape(SEQ_DEV, blocks, width, KVH, HD)
    new_keys = appended[:, :, 0].astype(jnp.float32)
    new_values = appended[:, :, 1].astype(jnp.float32)
    scores = jnp.einsum('nskgd,spkd->nskgp', queries, cache_keys, precision=highest) * score_scale
    position = lax.broadcasted_iota(jnp.int32, (SEQ_DEV, CACHE), 1)
    usable = (position < limits[:, None])[None, :, None, None, :]
    scores = jnp.where(usable, scores, masked_score)
    shape_blocks = scores.shape[:4] + (blocks, width)
    scores = scores.reshape(shape_blocks)
    usable = jnp.broadcast_to(usable, scores.shape[:4] + (CACHE,)).reshape(shape_blocks)
    block_maxima = lax.optimization_barrier(jnp.max(scores, axis=5))
    recent = jnp.einsum('nskgd,mskd->nskgm', queries, new_keys, precision=highest) * score_scale
    ordering = lax.broadcasted_iota(jnp.int32, (STEPS, STEPS), 0)
    later = lax.broadcasted_iota(jnp.int32, (STEPS, STEPS), 1)
    causal = (ordering >= later)[:, None, None, None, :]
    recent = jnp.where(causal, recent, masked_score)
    maxima = jnp.maximum(lax.optimization_barrier(jnp.max(block_maxima, axis=4)), lax.optimization_barrier(jnp.max(recent, axis=4)))
    weights = jnp.where(usable, jnp.exp(scores - block_maxima[..., None]), 0.0)
    block_scale = jnp.exp(block_maxima - maxima[..., None])
    fresh_weights = jnp.exp(recent - maxima[..., None])
    totals = lax.optimization_barrier(jnp.sum(lax.optimization_barrier(jnp.sum(weights, axis=5)) * block_scale, axis=4)) + lax.optimization_barrier(jnp.sum(fresh_weights, axis=4))
    rounded = lax.optimization_barrier(weights.astype(jnp.bfloat16)).astype(jnp.float32)
    fresh_rounded = lax.optimization_barrier(fresh_weights.astype(jnp.bfloat16)).astype(jnp.float32)
    per_block = jnp.einsum('nskgjw,sjwkd->nskgjd', rounded, cache_values, precision=highest)
    combined = lax.optimization_barrier(jnp.sum(per_block * block_scale[..., None], axis=4))
    combined = combined + jnp.einsum('nskgm,mskd->nskgd', fresh_rounded, new_values, precision=highest)
    return (combined / totals[..., None]).astype(jnp.bfloat16)

def reference(hidden_in, norm_gain, w_query, w_keyval, w_out, query_input_factor, b_query, a_out, b_out, component_owner_rows, lengths, kv_cache):
    paired_rows = pairing_order(component_owner_rows, ADAPTER_RANK) * adapter_scale
    lifted_query = jnp.dot(paired_rows, b_query.astype(jnp.float32), precision=highest)
    merged_query = w_query.astype(jnp.float32) + jnp.dot(query_input_factor.astype(jnp.float32).T, lifted_query, precision=highest)
    lifted_out = jnp.dot(paired_rows, b_out.astype(jnp.float32), precision=highest)
    merged_out = w_out.astype(jnp.float32) + jnp.dot(a_out.astype(jnp.float32).T, lifted_out, precision=highest)
    flattened = hidden_in.astype(jnp.float32).reshape(STEPS * SEQS, D)
    spread = lax.rsqrt(lax.optimization_barrier(jnp.mean(flattened * flattened, axis=1, keepdims=True)) + norm_eps)
    normed = (flattened * spread * norm_gain).astype(jnp.bfloat16)
    normed_wide = normed.astype(jnp.float32)
    queries = jnp.dot(normed_wide, merged_query, precision=highest).astype(jnp.bfloat16)
    keyvals = jnp.dot(normed_wide, w_keyval.astype(jnp.float32).T, precision=highest).astype(jnp.bfloat16)
    groups = SEQS // SEQ_DEV
    head_rows = queries.reshape(STEPS, groups, SEQ_DEV, KVH, HQ // KVH, HD).transpose(1, 0, 2, 3, 4, 5)
    appended = keyvals.reshape(STEPS, groups, SEQ_DEV, 2, KVH, HD).transpose(1, 0, 2, 3, 4, 5)
    cached = kv_cache.reshape(groups, SEQ_DEV, CACHE, 2, KVH, HD)
    limits = lengths.reshape(groups, SEQ_DEV)
    mixed = lax.map(attend, (head_rows, appended, cached, limits))
    mixed = mixed.transpose(1, 0, 2, 3, 4, 5).reshape(STEPS * SEQS, HQ * HD)
    result = jnp.dot(mixed.astype(jnp.float32), merged_out, precision=highest)
    return result.reshape(STEPS, SEQS, D).astype(jnp.bfloat16)
```

```python
import jax
import jax.numpy as jnp
from jax import lax
from jax.experimental import pallas as pl
from jax.experimental.pallas import tpu as pltpu
from jax.sharding import PartitionSpec as P

HQ = 32
KVH = 4
HD = 128
STEPS = 4
SEQ = 8
D = 2560
NT = 16
NR = 32
RANK = 64
FEAT = D // NT
TOK = STEPS * SEQ
POS = 128
ROWS = TOK * 2
GROUP = HQ // KVH
CHUNKS = D // 128

adapter_scale = 2.0
norm_eps = 1e-06
masked_score = -1e30

F32 = jnp.float32
BF16 = jnp.bfloat16
MESH = pl.DeviceIdType.MESH


def dot(a, b):
    return jnp.dot(a, b, preferred_element_type=F32)


def dot_nt(a, b):
    return lax.dot_general(a, b, (((1,), (1,)), ((), ())), preferred_element_type=F32)


def split(x):
    hi = x.astype(BF16)
    return hi, (x - hi.astype(F32)).astype(BF16)


def iota(shape, dim):
    return lax.broadcasted_iota(jnp.int32, shape, dim)


def kernel(
    hid_hbm, gain_hbm, wq_hbm, wkv_hbm, wo_hbm, qif_hbm, bq_hbm, ao_hbm, bo_hbm, own_hbm, len_hbm, kv_hbm,
    out_ref,
    hid, gain, wq, wkv, wo, wide, narrow, own, lens, kv,
    hid_all, asm, pack, ad_send, ad_all, ad_f32, qi_mat, bq_mat, ao_mat, bo_mat,
    qf32, q_send, q_all, fresh_send, fresh_all,
    o_send, o_all, st_mat, st_send, st_all, mix, part, e_send, e_all,
    ld, own_sem, b_s, b_r, a_s, a_r, q_s, q_r, f_s, f_r, o_s, o_r, t_s, t_r, e_s, e_r,
):
    t = lax.axis_index("tensor")
    r = lax.axis_index("replica")

    def loads():
        pairs = [
            (hid_hbm, hid), (qif_hbm, wide.at[0]), (bq_hbm, narrow.at[0]), (ao_hbm, narrow.at[1]), (bo_hbm, wide.at[1]),
            (own_hbm, own), (len_hbm, lens), (gain_hbm, gain), (wq_hbm, wq), (wkv_hbm, wkv), (kv_hbm, kv), (wo_hbm, wo),
        ]
        return [pltpu.make_async_copy(a, b, ld.at[i]) for i, (a, b) in enumerate(pairs)]

    load = loads()
    for c in load:
        c.start()

    barrier = pltpu.get_barrier_semaphore()
    for d in range(1, NT):
        pl.semaphore_signal(barrier, inc=1, device_id={"tensor": lax.rem(t + d, NT)}, device_id_type=MESH)
    for d in range(1, NR):
        pl.semaphore_signal(barrier, inc=1, device_id={"replica": lax.rem(r + d, NR)}, device_id_type=MESH)

    for c in load[1:5]:
        c.wait()
    for j in range(2):
        pack[...] = jnp.zeros_like(pack)
        x = wide[j].astype(F32)
        for c in range(CHUNKS):
            pack[2 * c : 2 * c + 2, :] = x[:, 128 * c : 128 * c + 128]
        y = narrow[j].astype(F32)
        for c in range(2):
            pack[2 * (CHUNKS + c) : 2 * (CHUNKS + c) + 2, :] = y[:, 128 * c : 128 * c + 128]
        ad_send[j] = pack[...].astype(BF16)
    load[0].wait()
    pl.semaphore_wait(barrier, NT - 1 + NR - 1)

    sends = []

    def send_tensor(src, dst, ss, rs, d):
        peer = lax.rem(t + d, NT)
        c = pltpu.make_async_remote_copy(
            src_ref=src(peer), dst_ref=dst.at[t], send_sem=ss.at[d], recv_sem=rs.at[t],
            device_id={"tensor": peer}, device_id_type=MESH,
        )
        c.start()
        sends.append(c)

    far_first = [8, 7, 9, 6, 10, 5, 11, 4, 12, 3, 13, 2, 14, 1, 15]

    def send_all_tensor(src, dst, ss, rs):
        for d in far_first:
            send_tensor(src, dst, ss, rs, d)
        pltpu.make_async_copy(src(t), dst.at[t], rs.at[t]).start()

    def arrived(dst, rs, i):
        pltpu.make_async_copy(dst.at[i], dst.at[i], rs.at[i]).wait()

    def send_adapters(j):
        for d in range(1, NR):
            c = pltpu.make_async_remote_copy(
                src_ref=ad_send.at[j], dst_ref=ad_all.at[j, r], send_sem=a_s.at[j, d], recv_sem=a_r.at[j, r],
                device_id={"replica": lax.rem(r + d, NR)}, device_id_type=MESH,
            )
            c.start()
            sends.append(c)
        pltpu.make_async_copy(ad_send.at[j], ad_all.at[j, r], a_r.at[j, r]).start()

    def take_adapters(j, wide_mat, narrow_mat):
        for s in range(NR):
            arrived(ad_all.at[j], a_r.at[j], s)
        for s in range(NR):
            ad_f32[48 * s : 48 * s + 48, :] = ad_all[j, s].astype(F32)
        for c in range(CHUNKS + 2):
            rows = [ad_f32[pl.ds(2 * c + i, NR, stride=48), :] for i in range(2)]
            block = jnp.concatenate(rows, axis=0).astype(BF16)
            if c < CHUNKS:
                wide_mat[:, 128 * c : 128 * c + 128] = block
            else:
                narrow_mat[:, 128 * (c - CHUNKS) : 128 * (c - CHUNKS) + 128] = block

    send_all_tensor(lambda p: hid, hid_all, b_s, b_r)
    send_adapters(0)

    for c in load[5:]:
        c.wait()

    label = iota((RANK, RANK), 0)
    label = lax.rem(label, NR) * 2 + label // NR
    first = (label == own[0:1, :]).astype(F32).astype(BF16)
    second = (label == own[1:2, :]).astype(F32).astype(BF16)
    paired = (dot_nt(first, second) * adapter_scale).astype(BF16)

    squares = jnp.zeros((TOK, 1), F32)
    for s in range(NT):
        arrived(hid_all, b_r, s)
        x = hid_all[s].astype(F32)
        asm[:, FEAT * s : FEAT * (s + 1)] = x
        squares = squares + jnp.sum(x * x, axis=1, keepdims=True)
    spread = lax.rsqrt(squares * (1.0 / D) + norm_eps)
    normed = (asm[...] * spread * gain[...]).astype(BF16)

    queries = dot(normed, wq[...])
    fresh = dot_nt(normed, wkv[...]).astype(BF16).astype(F32)
    take_adapters(0, qi_mat, bq_mat)
    low_hi, low_lo = split(dot_nt(normed, qi_mat[...]))
    lifted = dot(paired, bq_mat[...]).astype(BF16)
    queries = queries + (dot(low_hi, lifted) + dot(low_lo, lifted))

    for n in range(STEPS):
        for h in range(2):
            qf32[pl.ds(n * 2 + h, SEQ, stride=8), :] = queries[n * SEQ : (n + 1) * SEQ, h * HD : (h + 1) * HD]
    q_send[...] = qf32[...].astype(BF16)
    send_all_tensor(lambda p: q_send, q_all, q_s, q_r)

    zeros = jnp.zeros((TOK, 64), F32)
    left = jnp.concatenate([fresh, zeros], axis=1)
    right = jnp.concatenate([zeros, fresh], axis=1)
    half = lax.rem(t, 2)
    fresh_send[...] = jnp.where(half == 0, left, right).astype(BF16)
    slot = (t // 8) * 2 + half
    head_row = lax.rem(t, 8) // 2
    for y in range(4):
        peer = head_row * 4 + y
        remote = pltpu.make_async_remote_copy(
            src_ref=fresh_send, dst_ref=fresh_all.at[slot], send_sem=f_s.at[y], recv_sem=f_r.at[slot],
            device_id={"tensor": peer}, device_id_type=MESH,
        )
        local = pltpu.make_async_copy(fresh_send, fresh_all.at[slot], f_r.at[slot])

        @pl.when(peer != t)
        def _():
            remote.start()

        @pl.when(peer == t)
        def _():
            local.start()

    send_adapters(1)

    lane = iota((4 * 16, 2 * POS), 1)
    row = iota((4 * 16, 2 * POS), 0)
    same = (lane // POS) == (lax.rem(row, 16) // 8)
    position = lax.rem(lane, POS) + t * POS
    stat_lane = iota((16, 128), 1)
    usables = []
    for p in range(4):
        limit = jnp.where(lane < POS, lens[2 * p], lens[2 * p + 1])
        usables.append(same & (position < limit))
    maxes = [jnp.full((16, 128), masked_score, F32) for _ in range(4)]
    sums = [jnp.zeros((16, 128), F32) for _ in range(4)]
    score_scale = HD ** (-0.5)
    for k in range(KVH):
        for y in range(4):
            arrived(q_all, q_r, 4 * k + y)
        for p in range(4):
            usable = usables[p]
            lhs = jnp.concatenate([q_all[4 * k + y, 16 * p : 16 * p + 16, :] for y in range(4)], axis=0)
            keys = kv[2 * p : 2 * p + 2, :, HD * k : HD * (k + 1)].reshape(2 * POS, HD)
            values = kv[2 * p : 2 * p + 2, :, HD * (KVH + k) : HD * (KVH + k + 1)].reshape(2 * POS, HD)
            scores = jnp.where(usable, dot_nt(lhs, keys) * score_scale, masked_score)
            top = jnp.max(scores, axis=1, keepdims=True)
            weights = jnp.where(usable, jnp.exp(scores - top), 0.0)
            total = jnp.sum(weights, axis=1, keepdims=True)
            mixed = dot(weights.astype(BF16), values).astype(BF16)
            for y in range(4):
                i = 4 * k + y
                o_send[i, 16 * p : 16 * p + 16, :] = mixed[16 * y : 16 * y + 16, :]
                maxes[p] = jnp.where(stat_lane == i, top[16 * y : 16 * y + 16, :], maxes[p])
                sums[p] = jnp.where(stat_lane == i, total[16 * y : 16 * y + 16, :], sums[p])
    for p in range(4):
        st_mat[16 * p : 16 * p + 16, :] = maxes[p]
        st_mat[64 + 16 * p : 64 + 16 * p + 16, :] = sums[p]
    stats = jnp.transpose(st_mat[...])
    for i in range(NT):
        st_send[i] = stats[i : i + 1, :]
    send_all_tensor(lambda p: st_send.at[p], st_all, t_s, t_r)
    send_all_tensor(lambda p: o_send.at[p], o_all, o_s, o_r)

    for j in range(4):
        arrived(fresh_all, f_r, j)
    new_keys = fresh_all[0] + fresh_all[1]
    new_values = fresh_all[2] + fresh_all[3]
    row = iota((ROWS, TOK), 0)
    col = iota((ROWS, TOK), 1)
    causal = (lax.rem(col, SEQ) == row // 8) & (col // SEQ <= lax.rem(row, 8) // 2)
    recent = jnp.where(causal, dot_nt(q_send[...], new_keys) * score_scale, masked_score)
    recent_top = jnp.max(recent, axis=1, keepdims=True)

    take_adapters(1, bo_mat, ao_mat)
    lifted_out = dot(paired, bo_mat[...]).astype(BF16)

    for i in range(NT):
        arrived(st_all, t_r, i)
    st_mat[...] = jnp.full_like(st_mat, masked_score)
    for i in range(NT):
        st_mat[i : i + 1, :] = st_all[i]
    stats = jnp.transpose(st_mat[...])
    tops = stats[0:ROWS, :]
    valid = iota((ROWS, 128), 1) < NT
    totals = jnp.where(valid, stats[ROWS : 2 * ROWS, :], 0.0)
    peak = jnp.maximum(jnp.max(tops, axis=1, keepdims=True), recent_top)
    factor = jnp.where(valid, jnp.exp(tops - peak), 0.0)
    recent_weights = jnp.where(causal, jnp.exp(recent - peak), 0.0)
    total = jnp.sum(totals * factor, axis=1, keepdims=True) + jnp.sum(recent_weights, axis=1, keepdims=True)
    acc = dot(recent_weights.astype(BF16), new_values)
    for i in range(NT):
        arrived(o_all, o_r, i)
        acc = acc + o_all[i].astype(F32) * factor[:, i : i + 1]
    mix[...] = acc / total
    mixed = jnp.concatenate(
        [
            jnp.concatenate([mix[pl.ds(n * 2 + h, SEQ, stride=8), :] for h in range(2)], axis=1)
            for n in range(STEPS)
        ],
        axis=0,
    ).astype(BF16)

    low_hi, low_lo = split(dot_nt(mixed, ao_mat[...]))
    part[...] = dot(mixed, wo[...]) + (dot(low_hi, lifted_out) + dot(low_lo, lifted_out))
    for i in range(NT):
        e_send[i] = part[:, FEAT * i : FEAT * (i + 1)].astype(BF16)
    send_all_tensor(lambda p: e_send.at[p], e_all, e_s, e_r)
    summed = jnp.zeros((TOK, FEAT), F32)
    for i in range(NT):
        arrived(e_all, e_r, i)
        summed = summed + e_all[i].astype(F32)
    out_ref[...] = summed.astype(BF16)

    for c in sends:
        c.wait_send()
    for y in range(4):
        peer = head_row * 4 + y
        remote = pltpu.make_async_remote_copy(
            src_ref=fresh_send, dst_ref=fresh_all.at[slot], send_sem=f_s.at[y], recv_sem=f_r.at[slot],
            device_id={"tensor": peer}, device_id_type=MESH,
        )

        @pl.when(peer != t)
        def _():
            remote.wait_send()


def body(
    hidden_in, norm_gain, w_query, w_keyval, w_out, query_input_factor, b_query, a_out, b_out,
    component_owner_rows, lengths, kv_cache,
):
    dma = pltpu.SemaphoreType.DMA
    vmem = pltpu.VMEM
    scratch = [
        vmem((TOK, FEAT), BF16),
        vmem((1, D), F32),
        vmem((D, 256), BF16),
        vmem((64, D), BF16),
        vmem((256, D), BF16),
        vmem((2, 2, D), BF16),
        vmem((2, 2, 256), BF16),
        vmem((2, RANK), jnp.int32),
        pltpu.SMEM((SEQ,), jnp.int32),
        vmem((SEQ, POS, 1024), BF16),
        vmem((NT, TOK, FEAT), BF16),
        vmem((TOK, D), F32),
        vmem((48, 128), F32),
        vmem((2, 48, 128), BF16),
        vmem((2, NR, 48, 128), BF16),
        vmem((NR * 48, 128), F32),
        vmem((RANK, D), BF16),
        vmem((RANK, 256), BF16),
        vmem((RANK, 256), BF16),
        vmem((RANK, D), BF16),
        vmem((ROWS, HD), F32),
        vmem((ROWS, HD), BF16),
        vmem((NT, ROWS, HD), BF16),
        vmem((TOK, 128), BF16),
        vmem((4, TOK, 128), BF16),
        vmem((NT, ROWS, HD), BF16),
        vmem((NT, ROWS, HD), BF16),
        vmem((128, 128), F32),
        vmem((NT, 1, 128), F32),
        vmem((NT, 1, 128), F32),
        vmem((ROWS, HD), F32),
        vmem((TOK, D), F32),
        vmem((NT, TOK, FEAT), BF16),
        vmem((NT, TOK, FEAT), BF16),
        dma((12,)), dma((1,)),
        dma((NT,)), dma((NT,)),
        dma((2, NR)), dma((2, NR)),
        dma((NT,)), dma((NT,)),
        dma((4,)), dma((4,)),
        dma((NT,)), dma((NT,)),
        dma((NT,)), dma((NT,)),
        dma((NT,)), dma((NT,)),
    ]
    out = pl.pallas_call(
        kernel,
        out_shape=jax.ShapeDtypeStruct((TOK, FEAT), BF16),
        in_specs=[pl.BlockSpec(memory_space=pltpu.HBM)] * 12,
        out_specs=pl.BlockSpec(memory_space=pltpu.VMEM),
        scratch_shapes=scratch,
        compiler_params=pltpu.CompilerParams(collective_id=0, has_side_effects=True, vmem_limit_bytes=48 << 20),
    )(
        hidden_in.reshape(TOK, FEAT), norm_gain.reshape(1, D), w_query, w_keyval, w_out, query_input_factor, b_query,
        a_out, b_out, component_owner_rows, lengths, kv_cache,
    )
    return out.reshape(STEPS, SEQ, FEAT)


def solution(mesh):
    return jax.shard_map(
        body,
        mesh=mesh,
        in_specs=(
            P(None, "replica", "tensor"),
            P(),
            P(None, "tensor"),
            P("tensor", None),
            P("tensor", None),
            P("replica", None),
            P("replica", "tensor"),
            P("replica", "tensor"),
            P("replica", None),
            P(),
            P("replica"),
            P("replica", "tensor", None),
        ),
        out_specs=P(None, "replica", "tensor"),
        check_vma=False,
    )
```

```python
import jax
import jax.numpy as jnp
from jax import lax
from jax.experimental import pallas as pl
from jax.experimental.pallas import tpu as pltpu
from jax.sharding import PartitionSpec as P

HQ = 32
KVH = 4
HD = 128
STEPS = 4
SEQ = 8
D = 2560
NT = 16
NR = 32
RANK = 64
FEAT = D // NT
TOK = STEPS * SEQ
POS = 128
ROWS = TOK * 2
GROUP = HQ // KVH
CHUNKS = D // 128

adapter_scale = 2.0
norm_eps = 1e-06
masked_score = -1e30

F32 = jnp.float32
BF16 = jnp.bfloat16
MESH = pl.DeviceIdType.MESH


def dot(a, b):
    return jnp.dot(a, b, preferred_element_type=F32)


def dot_nt(a, b):
    return lax.dot_general(a, b, (((1,), (1,)), ((), ())), preferred_element_type=F32)


def split(x):
    hi = x.astype(BF16)
    return hi, (x - hi.astype(F32)).astype(BF16)


def iota(shape, dim):
    return lax.broadcasted_iota(jnp.int32, shape, dim)


def kernel(
    hid_hbm, gain_hbm, wq_hbm, wkv_hbm, wo_hbm, qif_hbm, bq_hbm, ao_hbm, bo_hbm, own_hbm, len_hbm, kv_hbm,
    out_ref,
    hid, gain, wq, wkv, wo, wide, narrow, own, lens, kv,
    hid_all, asm, pack, ad_send, ad_all, ad_f32, qi_mat, bq_mat, ao_mat, bo_mat,
    qf32, q_send, q_all, fresh_send, fresh_all,
    o_send, o_all, st_mat, st_send, st_all, mix, e_send, e_mid, e_comb, e_near, e_far,
    ld, b_s, b_r, a_s, a_r, x_s, x_r, k_s, k_r, q_s, q_r, f_s, f_r, o_s, o_r, t_s, t_r, e_s, m_r, n_s, n_r, far_r,
):
    t = lax.axis_index("tensor")
    r = lax.axis_index("replica")
    z = t // 4
    y = lax.rem(t, 4)
    zs = [z] + [lax.rem(z + d, 4) for d in range(1, 4)]
    ys = [y] + [lax.rem(y + d, 4) for d in range(1, 4)]

    pairs = [
        (hid_hbm, hid), (qif_hbm, wide.at[0]), (bq_hbm, narrow.at[0]), (ao_hbm, narrow.at[1]), (bo_hbm, wide.at[1]),
        (own_hbm, own), (len_hbm, lens), (gain_hbm, gain), (wq_hbm, wq), (wkv_hbm, wkv), (wo_hbm, wo),
    ]
    load = [pltpu.make_async_copy(a, b, ld.at[i]) for i, (a, b) in enumerate(pairs)]
    for c in load:
        c.start()

    barrier = pltpu.get_barrier_semaphore()
    near = lax.rem(r, 8)
    replica_peers = [r - near + lax.rem(near + d, 8) for d in range(1, 8)]
    replica_peers += [lax.rem(r + 8 * d, NR) for d in range(1, 4)]
    for d in range(1, NT):
        pl.semaphore_signal(barrier, inc=1, device_id={"tensor": lax.rem(t + d, NT)}, device_id_type=MESH)
    for peer in replica_peers:
        pl.semaphore_signal(barrier, inc=1, device_id={"replica": peer}, device_id_type=MESH)

    for c in load[1:5]:
        c.wait()
    for j in range(2):
        pack[...] = jnp.zeros_like(pack)
        x = wide[j].astype(F32)
        for c in range(CHUNKS):
            pack[2 * c : 2 * c + 2, :] = x[:, 128 * c : 128 * c + 128]
        w = narrow[j].astype(F32)
        for c in range(2):
            pack[2 * (CHUNKS + c) : 2 * (CHUNKS + c) + 2, :] = w[:, 128 * c : 128 * c + 128]
        ad_send[j] = pack[...].astype(BF16)
    load[0].wait()
    pl.semaphore_wait(barrier, NT - 1 + len(replica_peers))

    sends = []

    def remote(src, dst, ss, rs, peer, axis="tensor"):
        c = pltpu.make_async_remote_copy(
            src_ref=src, dst_ref=dst, send_sem=ss, recv_sem=rs, device_id={axis: peer}, device_id_type=MESH
        )
        c.start()
        sends.append(c)

    maybe = []

    def anywhere(src, dst, ss, rs, peer):
        c = pltpu.make_async_remote_copy(
            src_ref=src, dst_ref=dst, send_sem=ss, recv_sem=rs, device_id={"tensor": peer}, device_id_type=MESH
        )

        @pl.when(peer != t)
        def _():
            c.start()

        @pl.when(peer == t)
        def _():
            pltpu.make_async_copy(src, dst, rs).start()

        maybe.append((peer, c))

    def arrived(ref, sem):
        pltpu.make_async_copy(ref, ref, sem).wait()

    for d in (2, 1, 3, 0):
        remote(hid, hid_all.at[t], b_s.at[d], b_r.at[t], zs[2] * 4 + ys[d])
    for d in (1, 3):
        remote(hid, hid_all.at[t], b_s.at[3 + d], b_r.at[t], zs[d] * 4 + y)
    for d in (2, 1, 3):
        remote(hid, hid_all.at[t], b_s.at[6 + d], b_r.at[t], z * 4 + ys[d])
    pltpu.make_async_copy(hid, hid_all.at[t], b_r.at[t]).start()

    def adapters_near(j):
        for d in range(1, 8):
            peer = r - near + lax.rem(near + d, 8)
            remote(ad_send.at[j], ad_all.at[j, r], a_s.at[j, d], a_r.at[j, near], peer, "replica")
        pltpu.make_async_copy(ad_send.at[j], ad_all.at[j, r], a_r.at[j, near]).start()

    def adapters_across(j):
        base = r - near
        for s in range(8):
            arrived(ad_all.at[j, base + s], a_r.at[j, s])
        mine = ad_all.at[j, pl.ds(base, 8)]
        for d in (2, 1, 3):
            remote(mine, mine, x_s.at[j, d], x_r.at[j, r // 8], lax.rem(r + 8 * d, NR), "replica")

    def take_adapters(j, wide_mat, narrow_mat):
        for d in range(1, 4):
            group = lax.rem(r // 8 + d, 4)
            arrived(ad_all.at[j, pl.ds(group * 8, 8)], x_r.at[j, group])
        for s in range(NR):
            ad_f32[48 * s : 48 * s + 48, :] = ad_all[j, s].astype(F32)
        for c in range(CHUNKS + 2):
            rows = [ad_f32[pl.ds(2 * c + i, NR, stride=48), :] for i in range(2)]
            block = jnp.concatenate(rows, axis=0).astype(BF16)
            if c < CHUNKS:
                wide_mat[:, 128 * c : 128 * c + 128] = block
            else:
                narrow_mat[:, 128 * (c - CHUNKS) : 128 * (c - CHUNKS) + 128] = block

    adapters_near(0)

    for d in (2, 1, 3, 0):
        for j in range(2):
            src = kv_hbm.at[:, :, pl.ds(pl.multiple_of((j * KVH + ys[d]) * HD, HD), HD)]
            dst = kv.at[j, :, y]
            if d == 0:
                pltpu.make_async_copy(src, dst, k_r.at[j, y]).start()
            else:
                remote(src, dst, k_s.at[j, d], k_r.at[j, y], z * 4 + ys[d])

    for d in (1, 3):
        block = zs[d] * 4 + y
        arrived(hid_all.at[block], b_r.at[block])
        for e in (2, 1, 3):
            remote(hid_all.at[block], hid_all.at[block], b_s.at[8 + 2 * d + e], b_r.at[block], z * 4 + ys[e])

    adapters_across(0)
    adapters_near(1)

    for c in load[5:]:
        c.wait()

    label = iota((RANK, RANK), 0)
    label = lax.rem(label, NR) * 2 + label // NR
    first = (label == own[0:1, :]).astype(F32).astype(BF16)
    second = (label == own[1:2, :]).astype(F32).astype(BF16)
    paired = (dot_nt(first, second) * adapter_scale).astype(BF16)

    for e in range(4):
        for d in range(4):
            if e == 0 and d in (1, 3):
                continue
            block = zs[d] * 4 + ys[e]
            arrived(hid_all.at[block], b_r.at[block])
    squares = jnp.zeros((TOK, 1), F32)
    for s in range(NT):
        x = hid_all[s].astype(F32)
        asm[:, FEAT * s : FEAT * (s + 1)] = x
        squares = squares + jnp.sum(x * x, axis=1, keepdims=True)
    spread = lax.rsqrt(squares * (1.0 / D) + norm_eps)
    normed = jnp.concatenate(
        [
            (asm[:, 128 * c : 128 * c + 128] * spread * gain[c : c + 1, :]).astype(BF16)
            for c in range(CHUNKS)
        ],
        axis=1,
    )

    queries = dot(normed, wq[...])
    fresh = dot_nt(normed, wkv[...]).astype(BF16).astype(F32)
    take_adapters(0, qi_mat, bq_mat)
    low_hi, low_lo = split(dot_nt(normed, qi_mat[...]))
    lifted = dot(paired, bq_mat[...]).astype(BF16)
    queries = queries + (dot(low_hi, lifted) + dot(low_lo, lifted))

    for n in range(STEPS):
        for h in range(2):
            qf32[pl.ds(n * 2 + h, SEQ, stride=8), :] = queries[n * SEQ : (n + 1) * SEQ, h * HD : (h + 1) * HD]
    q_send[...] = qf32[...].astype(BF16)
    for d in (2, 1, 3, 0):
        anywhere(q_send, q_all.at[y], q_s.at[d], q_r.at[y], zs[d] * 4 + z)

    zeros = jnp.zeros((TOK, 64), F32)
    left = jnp.concatenate([fresh, zeros], axis=1)
    right = jnp.concatenate([zeros, fresh], axis=1)
    half = lax.rem(t, 2)
    fresh_send[...] = jnp.where(half == 0, left, right).astype(BF16)
    slot = (t // 8) * 2 + half
    head_row = lax.rem(t, 8) // 2
    for e in range(4):
        anywhere(fresh_send, fresh_all.at[slot], f_s.at[e], f_r.at[slot], head_row * 4 + e)

    adapters_across(1)

    score_scale = HD ** (-0.5)
    position = iota((GROUP * STEPS, 4 * POS), 1) + z * (4 * POS)
    usables = [position < lens[s] for s in range(SEQ)]
    for j in range(2):
        for e in range(4):
            arrived(kv.at[j, :, ys[e]], k_r.at[j, ys[e]])
    for e in range(4):
        arrived(q_all.at[e], q_r.at[e])
    rows = [q_all[e].astype(F32) for e in range(4)]
    scores = []
    for s in range(SEQ):
        lhs = jnp.concatenate([rows[e][8 * s : 8 * s + 8, :] for e in range(4)], axis=0).astype(BF16)
        keys = kv[0, s].reshape(4 * POS, HD)
        scores.append(jnp.where(usables[s], dot_nt(lhs, keys) * score_scale, masked_score))
    tops = [jnp.max(x, axis=1, keepdims=True) for x in scores]
    weights = [jnp.where(usables[s], jnp.exp(scores[s] - tops[s]), 0.0) for s in range(SEQ)]
    totals = [jnp.sum(x, axis=1, keepdims=True) for x in weights]
    values = [dot(weights[s].astype(BF16), kv[1, s].reshape(4 * POS, HD)) for s in range(SEQ)]
    lane = iota((2 * ROWS, 128), 1)
    stats = jnp.zeros((2 * ROWS, 128), F32)
    for e in range(4):
        part = slice(8 * e, 8 * e + 8)
        o_send[e] = jnp.concatenate([v[part, :] for v in values], axis=0).astype(BF16)
        column = jnp.concatenate([v[part, :] for v in tops] + [v[part, :] for v in totals], axis=0)
        stats = jnp.where(lane == e, column, stats)
    stats = jnp.transpose(stats)
    for e in range(4):
        st_send[e] = stats[e : e + 1, :]
    for e in range(4):
        anywhere(o_send.at[e], o_all.at[z], o_s.at[e], o_r.at[z], y * 4 + e)
        anywhere(st_send.at[e], st_all.at[z], t_s.at[e], t_r.at[z], y * 4 + e)

    for j in range(4):
        arrived(fresh_all.at[j], f_r.at[j])
    new_keys = fresh_all[0] + fresh_all[1]
    new_values = fresh_all[2] + fresh_all[3]
    row = iota((ROWS, TOK), 0)
    col = iota((ROWS, TOK), 1)
    causal = (lax.rem(col, SEQ) == row // 8) & (col // SEQ <= lax.rem(row, 8) // 2)
    recent = jnp.where(causal, dot_nt(q_send[...], new_keys) * score_scale, masked_score)
    recent_top = jnp.max(recent, axis=1, keepdims=True)

    take_adapters(1, bo_mat, ao_mat)
    lifted_out = dot(paired, bo_mat[...]).astype(BF16)
    wide_mat = qi_mat
    wide_mat[...] = lifted_out

    for d in range(4):
        arrived(st_all.at[d], t_r.at[d])
    st_mat[...] = jnp.full_like(st_mat, masked_score)
    for d in range(4):
        st_mat[d : d + 1, :] = st_all[d]
    stats = jnp.transpose(st_mat[...])
    valid = iota((ROWS, 128), 1) < 4
    tops = stats[0:ROWS, :]
    totals = jnp.where(valid, stats[ROWS : 2 * ROWS, :], 0.0)
    peak = jnp.maximum(jnp.max(tops, axis=1, keepdims=True), recent_top)
    factor = jnp.where(valid, jnp.exp(tops - peak), 0.0)
    recent_weights = jnp.where(causal, jnp.exp(recent - peak), 0.0)
    total = jnp.sum(totals * factor, axis=1, keepdims=True) + jnp.sum(recent_weights, axis=1, keepdims=True)
    acc = dot(recent_weights.astype(BF16), new_values)
    for d in range(4):
        arrived(o_all.at[d], o_r.at[d])
        acc = acc + o_all[d].astype(F32) * factor[:, d : d + 1]
    mix[...] = acc / total
    mixed = jnp.concatenate(
        [
            jnp.concatenate([mix[pl.ds(n * 2 + h, SEQ, stride=8), :] for h in range(2)], axis=1)
            for n in range(STEPS)
        ],
        axis=0,
    ).astype(BF16)

    low_hi, low_lo = split(dot_nt(mixed, ao_mat[...]))

    def project(d):
        cols = pl.ds(pl.multiple_of(zs[d] * (4 * FEAT), 128), 4 * FEAT)
        lifted = wide_mat[:, cols]
        block = dot(mixed, wo[:, cols]) + (dot(low_hi, lifted) + dot(low_lo, lifted))
        for e in range(4):
            e_send[4 * d + e] = block[:, FEAT * e : FEAT * (e + 1)].astype(BF16)

    project(2)
    for e in range(4):
        remote(e_send.at[8 + e], e_far.at[y], e_s.at[8 + e], far_r.at[y], zs[2] * 4 + e)
    for d in (1, 3, 0):
        project(d)
        for e in (2, 1, 3):
            remote(e_send.at[4 * d + ys[e]], e_mid.at[d, y], e_s.at[4 * d + e], m_r.at[d, y], z * 4 + ys[e])

    def along_y(d):
        total = e_send[4 * d + y].astype(F32)
        for e in (1, 3, 2):
            arrived(e_mid.at[d, ys[e]], m_r.at[d, ys[e]])
            total = total + e_mid[d, ys[e]].astype(F32)
        return total

    for d in (1, 3):
        e_comb[d] = along_y(d).astype(BF16)
        remote(e_comb.at[d], e_near.at[d], n_s.at[d], n_r.at[d], zs[d] * 4 + y)
    summed = along_y(0)
    for d in (1, 3):
        arrived(e_near.at[d], n_r.at[d])
        summed = summed + e_near[d].astype(F32)
    for e in range(4):
        arrived(e_far.at[e], far_r.at[e])
        summed = summed + e_far[e].astype(F32)
    out_ref[...] = summed.astype(BF16)

    for c in sends:
        c.wait_send()
    for peer, c in maybe:

        @pl.when(peer != t)
        def _():
            c.wait_send()


def body(
    hidden_in, norm_gain, w_query, w_keyval, w_out, query_input_factor, b_query, a_out, b_out,
    component_owner_rows, lengths, kv_cache,
):
    dma = pltpu.SemaphoreType.DMA
    vmem = pltpu.VMEM
    scratch = [
        vmem((TOK, FEAT), BF16),
        vmem((CHUNKS, 128), F32),
        vmem((D, 256), BF16),
        vmem((64, D), BF16),
        vmem((256, D), BF16),
        vmem((2, 2, D), BF16),
        vmem((2, 2, 256), BF16),
        vmem((2, RANK), jnp.int32),
        pltpu.SMEM((SEQ,), jnp.int32),
        vmem((2, SEQ, 4, POS, HD), BF16),
        vmem((NT, TOK, FEAT), BF16),
        vmem((TOK, D), F32),
        vmem((48, 128), F32),
        vmem((2, 48, 128), BF16),
        vmem((2, NR, 48, 128), BF16),
        vmem((NR * 48, 128), F32),
        vmem((RANK, D), BF16),
        vmem((RANK, 256), BF16),
        vmem((RANK, 256), BF16),
        vmem((RANK, D), BF16),
        vmem((ROWS, HD), F32),
        vmem((ROWS, HD), BF16),
        vmem((4, ROWS, HD), BF16),
        vmem((TOK, 128), BF16),
        vmem((4, TOK, 128), BF16),
        vmem((4, ROWS, HD), BF16),
        vmem((4, ROWS, HD), BF16),
        vmem((128, 128), F32),
        vmem((4, 1, 128), F32),
        vmem((4, 1, 128), F32),
        vmem((ROWS, HD), F32),
        vmem((NT, TOK, FEAT), BF16),
        vmem((4, 4, TOK, FEAT), BF16),
        vmem((4, TOK, FEAT), BF16),
        vmem((4, TOK, FEAT), BF16),
        vmem((4, TOK, FEAT), BF16),
        dma((11,)),
        dma((18,)), dma((NT,)),
        dma((2, 8)), dma((2, 8)),
        dma((2, 4)), dma((2, 4)),
        dma((2, 4)), dma((2, 4)),
        dma((4,)), dma((4,)),
        dma((4,)), dma((4,)),
        dma((4,)), dma((4,)),
        dma((4,)), dma((4,)),
        dma((NT,)), dma((4, 4)),
        dma((4,)), dma((4,)),
        dma((4,)),
    ]
    out = pl.pallas_call(
        kernel,
        out_shape=jax.ShapeDtypeStruct((TOK, FEAT), BF16),
        in_specs=[pl.BlockSpec(memory_space=pl.ANY)] * 12,
        out_specs=pl.BlockSpec(memory_space=pltpu.VMEM),
        scratch_shapes=scratch,
        compiler_params=pltpu.CompilerParams(collective_id=0, has_side_effects=True, vmem_limit_bytes=62 << 20),
    )(
        hidden_in.reshape(TOK, FEAT), norm_gain.reshape(CHUNKS, 128), w_query, w_keyval, w_out, query_input_factor, b_query,
        a_out, b_out, component_owner_rows, lengths, kv_cache,
    )
    return out.reshape(STEPS, SEQ, FEAT)


def solution(mesh):
    return jax.shard_map(
        body,
        mesh=mesh,
        in_specs=(
            P(None, "replica", "tensor"),
            P(),
            P(None, "tensor"),
            P("tensor", None),
            P("tensor", None),
            P("replica", None),
            P("replica", "tensor"),
            P("replica", "tensor"),
            P("replica", None),
            P(),
            P("replica"),
            P("replica", "tensor", None),
        ),
        out_specs=P(None, "replica", "tensor"),
        check_vma=False,
    )
```

```python
import jax
import jax.numpy as jnp
from jax import lax
from jax.experimental import pallas as pl
from jax.experimental.pallas import tpu as pltpu
from jax.sharding import PartitionSpec as P

HQ = 32
KVH = 4
HD = 128
STEPS = 4
SEQ = 8
D = 2560
NT = 16
NR = 32
RANK = 64
FEAT = D // NT
TOK = STEPS * SEQ
POS = 128
ROWS = TOK * 2
GROUP = HQ // KVH
CHUNKS = D // 128

adapter_scale = 2.0
norm_eps = 1e-06
masked_score = -1e30

F32 = jnp.float32
BF16 = jnp.bfloat16
MESH = pl.DeviceIdType.MESH


def dot(a, b):
    return jnp.dot(a, b, preferred_element_type=F32)


def dot_nt(a, b):
    return lax.dot_general(a, b, (((1,), (1,)), ((), ())), preferred_element_type=F32)


def split(x):
    hi = x.astype(BF16)
    return hi, (x - hi.astype(F32)).astype(BF16)


def iota(shape, dim):
    return lax.broadcasted_iota(jnp.int32, shape, dim)


def kernel(
    hid_hbm, gain_hbm, wq_hbm, wkv_hbm, wo_hbm, qif_hbm, bq_hbm, ao_hbm, bo_hbm, own_hbm, len_hbm, kv_hbm,
    out_ref,
    hid, gain, wq, wkv, wo, wide, narrow, own, lens, kv,
    hid_all, asm, pack, ad_send, ad_all, ad_f32, qi_mat, bq_mat, ao_mat, bo_mat,
    qf32, q_send, q_all, o_send, o_mid, o_comb, o_near, st_mat, mix, e_send, e_mid, e_comb, e_near, e_far,
    ld, b_s, b_r, a_s, a_r, x_s, x_r, q_s, q_r, o_s, om_r, on_s, on_r, e_s, m_r, n_s, n_r, far_r,
):
    t = lax.axis_index("tensor")
    r = lax.axis_index("replica")
    z = t // 4
    y = lax.rem(t, 4)
    zs = [z] + [lax.rem(z + d, 4) for d in range(1, 4)]
    ys = [y] + [lax.rem(y + d, 4) for d in range(1, 4)]

    pairs = [
        (hid_hbm, hid), (qif_hbm, wide.at[0]), (bq_hbm, narrow.at[0]), (ao_hbm, narrow.at[1]), (bo_hbm, wide.at[1]),
        (own_hbm, own), (len_hbm, lens), (gain_hbm, gain), (wq_hbm, wq), (wkv_hbm, wkv), (kv_hbm, kv), (wo_hbm, wo),
    ]
    load = [pltpu.make_async_copy(a, b, ld.at[i]) for i, (a, b) in enumerate(pairs)]
    for c in load:
        c.start()

    barrier = pltpu.get_barrier_semaphore()
    near = lax.rem(r, 8)
    replica_peers = [r - near + lax.rem(near + d, 8) for d in range(1, 8)]
    replica_peers += [lax.rem(r + 8 * d, NR) for d in range(1, 4)]
    tensor_peers = [zs[d] * 4 + ys[e] for d in (1, 3) for e in range(4)] + [z * 4 + ys[e] for e in range(1, 4)]
    for peer in tensor_peers:
        pl.semaphore_signal(barrier, inc=1, device_id={"tensor": peer}, device_id_type=MESH)
    for peer in replica_peers:
        pl.semaphore_signal(barrier, inc=1, device_id={"replica": peer}, device_id_type=MESH)

    for c in load[1:5]:
        c.wait()
    for j in range(2):
        pack[...] = jnp.zeros_like(pack)
        x = wide[j].astype(F32)
        for c in range(CHUNKS):
            pack[2 * c : 2 * c + 2, :] = x[:, 128 * c : 128 * c + 128]
        w = narrow[j].astype(F32)
        for c in range(2):
            pack[2 * (CHUNKS + c) : 2 * (CHUNKS + c) + 2, :] = w[:, 128 * c : 128 * c + 128]
        ad_send[j] = pack[...].astype(BF16)
    load[0].wait()
    pl.semaphore_wait(barrier, len(tensor_peers) + len(replica_peers))

    sends = []

    def remote(src, dst, ss, rs, peer, axis="tensor"):
        c = pltpu.make_async_remote_copy(
            src_ref=src, dst_ref=dst, send_sem=ss, recv_sem=rs, device_id={axis: peer}, device_id_type=MESH
        )
        c.start()
        sends.append(c)

    def arrived(ref, sem):
        pltpu.make_async_copy(ref, ref, sem).wait()

    for d in (1, 3):
        remote(hid, hid_all.at[t], b_s.at[d], b_r.at[t], zs[d] * 4 + y)
    for d in (2, 1, 3):
        remote(hid, hid_all.at[t], b_s.at[3 + d], b_r.at[t], z * 4 + ys[d])
    pltpu.make_async_copy(hid, hid_all.at[t], b_r.at[t]).start()

    def adapters_near(j):
        for d in range(1, 8):
            peer = r - near + lax.rem(near + d, 8)
            remote(ad_send.at[j], ad_all.at[j, r], a_s.at[j, d], a_r.at[j, near], peer, "replica")
        pltpu.make_async_copy(ad_send.at[j], ad_all.at[j, r], a_r.at[j, near]).start()

    def adapters_across(j):
        base = r - near
        for s in range(8):
            arrived(ad_all.at[j, base + s], a_r.at[j, s])
        mine = ad_all.at[j, pl.ds(base, 8)]
        for d in (2, 1, 3):
            remote(mine, mine, x_s.at[j, d], x_r.at[j, r // 8], lax.rem(r + 8 * d, NR), "replica")

    def take_adapters(j, wide_mat, narrow_mat):
        for d in range(1, 4):
            group = lax.rem(r // 8 + d, 4)
            arrived(ad_all.at[j, pl.ds(group * 8, 8)], x_r.at[j, group])
        for s in range(NR):
            ad_f32[48 * s : 48 * s + 48, :] = ad_all[j, s].astype(F32)
        for c in range(CHUNKS + 2):
            rows = [ad_f32[pl.ds(2 * c + i, NR, stride=48), :] for i in range(2)]
            block = jnp.concatenate(rows, axis=0).astype(BF16)
            if c < CHUNKS:
                wide_mat[:, 128 * c : 128 * c + 128] = block
            else:
                narrow_mat[:, 128 * (c - CHUNKS) : 128 * (c - CHUNKS) + 128] = block

    adapters_near(0)

    for d in (1, 3):
        block = zs[d] * 4 + y
        held = hid_all.at[block]
        arrived(held, b_r.at[block])
        for e in (0, 1) if d == 1 else (2, 3):
            remote(held, held, b_s.at[4 + 4 * d + e], b_r.at[block], zs[4 - d] * 4 + ys[e])
        for e in (2, 1, 3):
            remote(held, held, b_s.at[19 + 3 * (d // 2) + e], b_r.at[block], z * 4 + ys[e])

    adapters_across(0)
    adapters_near(1)

    for c in load[5:]:
        c.wait()

    st_mat[...] = jnp.zeros_like(st_mat)
    label = iota((RANK, RANK), 0)
    label = lax.rem(label, NR) * 2 + label // NR
    first = (label == own[0:1, :]).astype(F32).astype(BF16)
    second = (label == own[1:2, :]).astype(F32).astype(BF16)
    paired = (dot_nt(first, second) * adapter_scale).astype(BF16)

    for e in range(4):
        for d in range(4):
            if e == 0 and d in (1, 3):
                continue
            block = zs[d] * 4 + ys[e]
            arrived(hid_all.at[block], b_r.at[block])
    squares = jnp.zeros((TOK, 1), F32)
    for s in range(NT):
        x = hid_all[s].astype(F32)
        asm[:, FEAT * s : FEAT * (s + 1)] = x
        squares = squares + jnp.sum(x * x, axis=1, keepdims=True)
    spread = lax.rsqrt(squares * (1.0 / D) + norm_eps)
    normed = jnp.concatenate(
        [
            (asm[:, 128 * c : 128 * c + 128] * spread * gain[c : c + 1, :]).astype(BF16)
            for c in range(CHUNKS)
        ],
        axis=1,
    )

    queries = dot(normed, wq[...])
    fresh = dot_nt(normed, wkv[...]).astype(BF16).astype(F32)
    take_adapters(0, qi_mat, bq_mat)
    low_hi, low_lo = split(dot_nt(normed, qi_mat[...]))
    lifted = dot(paired, bq_mat[...]).astype(BF16)
    queries = queries + (dot(low_hi, lifted) + dot(low_lo, lifted))

    for n in range(STEPS):
        for h in range(2):
            qf32[pl.ds(n * 2 + h, SEQ, stride=8), :] = queries[n * SEQ : (n + 1) * SEQ, h * HD : (h + 1) * HD]
    q_send[0:ROWS, :] = qf32[...].astype(BF16)
    q_send[ROWS : ROWS + 16, :] = jnp.concatenate([fresh[0:16, :], fresh[16:32, :]], axis=1).astype(BF16)
    for d in (2, 1, 3):
        remote(q_send, q_all.at[t], q_s.at[d], q_r.at[t], zs[d] * 4 + y)
    for e in (2, 1, 3):
        remote(q_send, q_all.at[t], q_s.at[3 + e], q_r.at[t], z * 4 + ys[e])
    pltpu.make_async_copy(q_send, q_all.at[t], q_r.at[t]).start()

    def hand_on(d):
        block = zs[d] * 4 + y
        held = q_all.at[block]
        arrived(held, q_r.at[block])
        for e in (2, 1, 3):
            remote(held, held, q_s.at[4 + 3 * d + e - 1], q_r.at[block], z * 4 + ys[e])

    adapters_across(1)

    score_scale = HD ** (-0.5)
    position = iota((GROUP * STEPS, POS), 1) + t * POS
    usables = [position < lens[s] for s in range(SEQ)]
    lane = iota((2 * ROWS, 128), 1)

    def put(ref, out, row):
        high = row.astype(BF16)
        rest = row - high.astype(F32)
        middle = rest.astype(BF16)
        low = (rest - middle.astype(F32)).astype(BF16)
        ref[0:ROWS, :] = out.astype(BF16)
        pieces = [high.astype(F32), middle.astype(F32), low.astype(F32), jnp.zeros((13, 128), F32)]
        ref[ROWS : ROWS + 16, :] = jnp.concatenate(pieces, axis=0).astype(BF16)

    def get(ref):
        pieces = ref[ROWS : ROWS + 16, :].astype(F32)
        return ref[0:ROWS, :].astype(F32), pieces[0:1, :] + pieces[1:2, :] + pieces[2:3, :]

    def attend(d):
        k = zs[d]
        rows = [q_all[4 * k + e, 0:ROWS, :].astype(F32) for e in range(4)]
        key_lanes = pl.ds(pl.multiple_of(k * HD, HD), HD)
        value_lanes = pl.ds(pl.multiple_of((KVH + k) * HD, HD), HD)
        scores = []
        for s in range(SEQ):
            lhs = jnp.concatenate([rows[e][8 * s : 8 * s + 8, :] for e in range(4)], axis=0).astype(BF16)
            scores.append(jnp.where(usables[s], dot_nt(lhs, kv[s, :, key_lanes]) * score_scale, masked_score))
        tops = [jnp.max(x, axis=1, keepdims=True) for x in scores]
        weights = [jnp.where(usables[s], jnp.exp(scores[s] - tops[s]), 0.0) for s in range(SEQ)]
        totals = [jnp.sum(x, axis=1, keepdims=True) for x in weights]
        values = [dot(weights[s].astype(BF16), kv[s, :, value_lanes]) for s in range(SEQ)]
        stats = jnp.zeros((2 * ROWS, 128), F32)
        for e in range(4):
            part = slice(8 * e, 8 * e + 8)
            column = jnp.concatenate([v[part, :] for v in tops] + [v[part, :] for v in totals], axis=0)
            stats = jnp.where(lane == e, column, stats)
        stats = jnp.transpose(stats)
        for e in range(4):
            part = slice(8 * e, 8 * e + 8)
            put(o_send.at[d, e], jnp.concatenate([v[part, :] for v in values], axis=0), stats[e : e + 1, :])
        for e in (2, 1, 3):
            remote(o_send.at[d, ys[e]], o_mid.at[d, y], o_s.at[d, e], om_r.at[d, y], z * 4 + ys[e])

    def take_queries(d):
        for e in range(0 if d == 0 else 1, 4):
            block = zs[d] * 4 + ys[e]
            arrived(q_all.at[block], q_r.at[block])

    take_queries(0)
    attend(0)
    hand_on(1)
    hand_on(3)
    hand_on(2)
    take_queries(1)
    attend(1)
    take_queries(3)
    attend(3)
    take_queries(2)
    attend(2)

    def along_y_values(d):
        for e in range(1, 4):
            arrived(o_mid.at[d, ys[e]], om_r.at[d, ys[e]])
        return [get(o_send.at[d, y])] + [get(o_mid.at[d, ys[e]]) for e in range(1, 4)]

    row_lane = iota((1, 128), 1)
    for d in (1, 3, 2):
        parts = along_y_values(d)
        rows = [row for _, row in parts]
        top = jnp.maximum(jnp.maximum(rows[0], rows[1]), jnp.maximum(rows[2], rows[3]))
        factors = [jnp.exp(row - top) for row in rows]
        total = sum(f * pltpu.roll(row, ROWS, 1) for f, row in zip(factors, rows))
        st_mat[0:4, :] = jnp.concatenate(factors, axis=0)
        columns = jnp.transpose(st_mat[...])
        acc = sum(parts[i][0] * columns[0:ROWS, i : i + 1] for i in range(4))
        put(o_comb.at[d], acc, jnp.where(row_lane < ROWS, top, pltpu.roll(total, ROWS, 1)))
        remote(o_comb.at[d], o_near.at[d], on_s.at[d], on_r.at[d], zs[d] * 4 + y)

    def halves(first):
        a = q_all[first, ROWS : ROWS + 16, :].astype(F32)
        b = q_all[first + 1, ROWS : ROWS + 16, :].astype(F32)
        upper = jnp.concatenate([a[:, 0:64], b[:, 0:64]], axis=1)
        lower = jnp.concatenate([a[:, 64:128], b[:, 64:128]], axis=1)
        return jnp.concatenate([upper, lower], axis=0).astype(BF16)

    new_keys = halves(2 * z)
    new_values = halves(8 + 2 * z)
    row = iota((ROWS, TOK), 0)
    col = iota((ROWS, TOK), 1)
    causal = (lax.rem(col, SEQ) == row // 8) & (col // SEQ <= lax.rem(row, 8) // 2)
    recent = jnp.where(causal, dot_nt(q_send[0:ROWS, :], new_keys) * score_scale, masked_score)
    recent_top = jnp.max(recent, axis=1, keepdims=True)

    take_adapters(1, bo_mat, ao_mat)
    lifted_out = dot(paired, bo_mat[...]).astype(BF16)
    wide_mat = qi_mat
    wide_mat[...] = lifted_out

    parts = along_y_values(0)
    for d in (1, 3, 2):
        arrived(o_near.at[d], on_r.at[d])
        parts.append(get(o_near.at[d]))
    count = len(parts)
    st_mat[0:count, :] = jnp.concatenate([row for _, row in parts], axis=0)
    stats = jnp.transpose(st_mat[...])
    valid = iota((ROWS, 128), 1) < count
    tops = jnp.where(valid, stats[0:ROWS, :], masked_score)
    totals = jnp.where(valid, stats[ROWS : 2 * ROWS, :], 0.0)
    peak = jnp.maximum(jnp.max(tops, axis=1, keepdims=True), recent_top)
    factor = jnp.where(valid, jnp.exp(tops - peak), 0.0)
    recent_weights = jnp.where(causal, jnp.exp(recent - peak), 0.0)
    total = jnp.sum(totals * factor, axis=1, keepdims=True) + jnp.sum(recent_weights, axis=1, keepdims=True)
    acc = dot(recent_weights.astype(BF16), new_values)
    for i in range(count):
        acc = acc + parts[i][0] * factor[:, i : i + 1]
    mix[...] = acc / total
    mixed = jnp.concatenate(
        [
            jnp.concatenate([mix[pl.ds(n * 2 + h, SEQ, stride=8), :] for h in range(2)], axis=1)
            for n in range(STEPS)
        ],
        axis=0,
    ).astype(BF16)

    low_hi, low_lo = split(dot_nt(mixed, ao_mat[...]))

    def project(d):
        cols = pl.ds(pl.multiple_of(zs[d] * (4 * FEAT), 128), 4 * FEAT)
        lifted = wide_mat[:, cols]
        block = dot(mixed, wo[:, cols]) + (dot(low_hi, lifted) + dot(low_lo, lifted))
        for e in range(4):
            e_send[4 * d + e] = block[:, FEAT * e : FEAT * (e + 1)].astype(BF16)

    project(2)
    for e in range(4):
        remote(e_send.at[8 + e], e_far.at[y], e_s.at[8 + e], far_r.at[y], zs[2] * 4 + e)
    for d in (1, 3, 0):
        project(d)
        for e in (2, 1, 3):
            remote(e_send.at[4 * d + ys[e]], e_mid.at[d, y], e_s.at[4 * d + e], m_r.at[d, y], z * 4 + ys[e])

    def along_y(d):
        total = e_send[4 * d + y].astype(F32)
        for e in (1, 3, 2):
            arrived(e_mid.at[d, ys[e]], m_r.at[d, ys[e]])
            total = total + e_mid[d, ys[e]].astype(F32)
        return total

    for d in (1, 3):
        e_comb[d] = along_y(d).astype(BF16)
        remote(e_comb.at[d], e_near.at[d], n_s.at[d], n_r.at[d], zs[d] * 4 + y)
    summed = along_y(0)
    for d in (1, 3):
        arrived(e_near.at[d], n_r.at[d])
        summed = summed + e_near[d].astype(F32)
    for e in range(4):
        arrived(e_far.at[e], far_r.at[e])
        summed = summed + e_far[e].astype(F32)
    out_ref[...] = summed.astype(BF16)

    for c in sends:
        c.wait_send()


def body(
    hidden_in, norm_gain, w_query, w_keyval, w_out, query_input_factor, b_query, a_out, b_out,
    component_owner_rows, lengths, kv_cache,
):
    dma = pltpu.SemaphoreType.DMA
    vmem = pltpu.VMEM
    scratch = [
        vmem((TOK, FEAT), BF16),
        vmem((CHUNKS, 128), F32),
        vmem((D, 256), BF16),
        vmem((64, D), BF16),
        vmem((256, D), BF16),
        vmem((2, 2, D), BF16),
        vmem((2, 2, 256), BF16),
        vmem((2, RANK), jnp.int32),
        pltpu.SMEM((SEQ,), jnp.int32),
        vmem((SEQ, POS, 1024), BF16),
        vmem((NT, TOK, FEAT), BF16),
        vmem((TOK, D), F32),
        vmem((48, 128), F32),
        vmem((2, 48, 128), BF16),
        vmem((2, NR, 48, 128), BF16),
        vmem((NR * 48, 128), F32),
        vmem((RANK, D), BF16),
        vmem((RANK, 256), BF16),
        vmem((RANK, 256), BF16),
        vmem((RANK, D), BF16),
        vmem((ROWS, HD), F32),
        vmem((ROWS + 16, HD), BF16),
        vmem((NT, ROWS + 16, HD), BF16),
        vmem((4, 4, ROWS + 16, HD), BF16),
        vmem((4, 4, ROWS + 16, HD), BF16),
        vmem((4, ROWS + 16, HD), BF16),
        vmem((4, ROWS + 16, HD), BF16),
        vmem((128, 128), F32),
        vmem((ROWS, HD), F32),
        vmem((NT, TOK, FEAT), BF16),
        vmem((4, 4, TOK, FEAT), BF16),
        vmem((4, TOK, FEAT), BF16),
        vmem((4, TOK, FEAT), BF16),
        vmem((4, TOK, FEAT), BF16),
        dma((12,)),
        dma((27,)), dma((NT,)),
        dma((2, 8)), dma((2, 8)),
        dma((2, 4)), dma((2, 4)),
        dma((NT,)), dma((NT,)),
        dma((4, 4)), dma((4, 4)),
        dma((4,)), dma((4,)),
        dma((NT,)), dma((4, 4)),
        dma((4,)), dma((4,)),
        dma((4,)),
    ]
    out = pl.pallas_call(
        kernel,
        out_shape=jax.ShapeDtypeStruct((TOK, FEAT), BF16),
        in_specs=[pl.BlockSpec(memory_space=pl.ANY)] * 12,
        out_specs=pl.BlockSpec(memory_space=pltpu.VMEM),
        scratch_shapes=scratch,
        compiler_params=pltpu.CompilerParams(collective_id=0, has_side_effects=True, vmem_limit_bytes=62 << 20),
    )(
        hidden_in.reshape(TOK, FEAT), norm_gain.reshape(CHUNKS, 128), w_query, w_keyval, w_out, query_input_factor, b_query,
        a_out, b_out, component_owner_rows, lengths, kv_cache,
    )
    return out.reshape(STEPS, SEQ, FEAT)


def solution(mesh):
    return jax.shard_map(
        body,
        mesh=mesh,
        in_specs=(
            P(None, "replica", "tensor"),
            P(),
            P(None, "tensor"),
            P("tensor", None),
            P("tensor", None),
            P("replica", None),
            P("replica", "tensor"),
            P("replica", "tensor"),
            P("replica", None),
            P(),
            P("replica"),
            P("replica", "tensor", None),
        ),
        out_specs=P(None, "replica", "tensor"),
        check_vma=False,
    )
```
